128 devices in a mesh: row: 8 (over z, core), col: 16 (over x, y).
Axes of the slice: x: 4, y: 4, z: 4, core: 2. Of those that a mesh axis runs over, the one named last changes fastest.
Arguments:
- features: bfloat16 [262144, 512], P(('row', 'col')), may hold values from -6 to 6
- history: bfloat16 [262144, 512], P(('row', 'col')), may hold values from -6 to 6
- cotangent: bfloat16 [262144, 512], P(('row', 'col')), may hold values from -0.03125 to 0.03125
- adjacency: bfloat16 [262144, 8, 128], P(('row', 'col')), as said below
- tile_source: int32 [2048, 8], P(('row', 'col')), may hold values from 0 to 39, as said below
- col_sends: int32 [128, 16, 1], P(('row', 'col')), may hold values from 0 to 15, as said below
- col_counts: int32 [128, 16], P(('row', 'col')), may hold values from 0 to 1, as said below
- row_sends: int32 [128, 8, 1], P(('row', 'col')), may hold values from 0 to 15, as said below
- row_counts: int32 [128, 8], P(('row', 'col')), may hold values from 0 to 1, as said below
- first_self: bfloat16 [512, 512], replicated, may hold values from -0.25 to 0.25
- first_neigh: bfloat16 [512, 512], replicated, may hold values from -1 to 1
- second_self: bfloat16 [512, 512], replicated, may hold values from -0.25 to 0.25
- second_neigh: bfloat16 [512, 512], replicated, may hold values from -1 to 1
Outputs:
- embeddings: bfloat16 [262144, 512], P(('row', 'col'))
- fresh_halo: bfloat16 [393216, 512], P(('row', 'col'))
- grad_first_self: float32 [512, 512], replicated
- grad_first_neigh: float32 [512, 512], replicated
- grad_second_self: float32 [512, 512], replicated
- grad_second_neigh: float32 [512, 512], replicated
The draws below stay inside these ranges and needn't reach their ends.
Inputs may be any that keep to these rules, and one draw needn't show every extreme that they name: col_counts[p, d] is 0 where d is p's own grid column. In every draw one partition receives 1 block from every other partition of its grid row and of its grid column. row_counts[p, d] is 0 where d is p's own grid row. `col_sends`: local block numbers of the sending partition. `row_sends`: local block numbers of the sending partition. `tile_source`: below 16: a local block; from 16 on: halo slot number plus 16. Only used halo slots are named. `adjacency`: Nonnegative; entry [n, 0, n mod 128] is positive for every node n.
All inputs are finite; a program needn't handle non-finite values.
Results may differ from the reference program's by a relative error of at most 0.0054.
Values may be sent and summed in bfloat16 or wider, within the bound.
A program may use at most 192 MiB of HBM per device.

```python
import math
import jax
import jax.numpy as jnp
from jax import lax

F = 512
H = 512
BLK = 128
TPB = 8
CAP = 1
NB = 16
LOC = 2048
NODES = 262144
NH = 24
HALO_ROWS = 393216
N_ROW = 8
N_COL = 16


def halo_counts(key):
    subkeys = jax.random.split(key, 7)
    crowded = jax.random.randint(subkeys[0], (N_ROW, N_COL), 0, 4, dtype=jnp.int32) == 0
    chosen_row = jax.random.randint(subkeys[1], (), 0, N_ROW, dtype=jnp.int32)
    chosen_col = jax.random.randint(subkeys[2], (), 0, N_COL, dtype=jnp.int32)
    grid_row = jnp.arange(N_ROW, dtype=jnp.int32)[:, None, None]
    owner_col = jnp.arange(N_COL, dtype=jnp.int32)[None, :, None]
    reader_col = jnp.arange(N_COL, dtype=jnp.int32)[None, None, :]
    shape_col = (N_ROW, N_COL, N_COL)
    sparse_col = jnp.where(jax.random.randint(subkeys[3], shape_col, 0, 4, dtype=jnp.int32) == 0, jax.random.randint(subkeys[4], shape_col, 1, CAP + 1, dtype=jnp.int32), 0)
    filled_col = crowded[grid_row, reader_col] | (grid_row == chosen_row) & (reader_col == chosen_col)
    by_col = jnp.where(filled_col, CAP, sparse_col)
    by_col = jnp.where(owner_col == reader_col, 0, by_col).astype(jnp.int32)
    owner_row = jnp.arange(N_ROW, dtype=jnp.int32)[:, None, None]
    grid_col = jnp.arange(N_COL, dtype=jnp.int32)[None, :, None]
    reader_row = jnp.arange(N_ROW, dtype=jnp.int32)[None, None, :]
    shape_row = (N_ROW, N_COL, N_ROW)
    sparse_row = jnp.where(jax.random.randint(subkeys[5], shape_row, 0, 4, dtype=jnp.int32) == 0, jax.random.randint(subkeys[6], shape_row, 1, CAP + 1, dtype=jnp.int32), 0)
    filled_row = crowded[reader_row, grid_col] | (reader_row == chosen_row) & (grid_col == chosen_col)
    by_row = jnp.where(filled_row, CAP, sparse_row)
    by_row = jnp.where(owner_row == reader_row, 0, by_row).astype(jnp.int32)
    return (by_col.reshape(N_ROW * N_COL, N_COL), by_row.reshape(N_ROW * N_COL, N_ROW))


def draw_col_counts(key, part):
    counts_pair = halo_counts(key)
    return counts_pair[0]


def draw_row_counts(key, part):
    counts_pair = halo_counts(key)
    return counts_pair[1]


def draw_col_sends(key, part):
    key = jax.random.fold_in(key, 2)
    return jax.random.randint(key, (N_ROW * N_COL, N_COL, CAP), 0, NB, dtype=jnp.int32)


def draw_row_sends(key, part):
    key = jax.random.fold_in(key, 3)
    return jax.random.randint(key, (N_ROW * N_COL, N_ROW, CAP), 0, NB, dtype=jnp.int32)


def draw_tile_source(key, part):
    col_counts, row_counts = halo_counts(key)
    key = jax.random.fold_in(key, 5)
    candidate = jax.random.randint(key, (N_ROW, N_COL, NB, TPB), 0, NB + NH, dtype=jnp.int32)
    grid_row = jnp.arange(N_ROW, dtype=jnp.int32)[:, None, None, None]
    grid_col = jnp.arange(N_COL, dtype=jnp.int32)[None, :, None, None]
    offset = candidate - NB
    in_col = (offset >= 0) & (offset < N_COL * CAP)
    col_owner = jnp.clip(offset // CAP, 0, N_COL - 1)
    col_slot = offset % CAP
    col_used = in_col & (col_slot < col_counts[grid_row * N_COL + col_owner, grid_col])
    second = offset - N_COL * CAP
    in_row = second >= 0
    row_owner = jnp.clip(second // CAP, 0, N_ROW - 1)
    row_slot = second % CAP
    row_used = in_row & (row_slot < row_counts[row_owner * N_COL + grid_col, grid_row])
    usable = (offset < 0) | col_used | row_used
    chosen = jnp.where(usable, candidate, candidate % NB)
    return chosen.reshape(N_ROW * N_COL * NB, TPB).astype(jnp.int32)


def draw_adjacency(key, part):
    key = jax.random.fold_in(key, 7)
    subkeys = jax.random.split(key, 4)
    low_density, high_density, column_top = (0.03, 0.3, 10.0)
    density = jnp.exp(jax.random.uniform(subkeys[0], (NODES, 1, 1), jnp.float32, math.log(low_density), math.log(high_density)))
    chance = jax.random.uniform(subkeys[1], (NODES, TPB, BLK), jnp.float32)
    strength = jnp.exp(jax.random.uniform(subkeys[2], (NODES, TPB, BLK), jnp.float32, math.log(0.5), math.log(2.0)))
    column_scale = jnp.exp(jax.random.uniform(subkeys[3], (NODES // BLK, 1, TPB, BLK), jnp.float32, 0.0, math.log(column_top)))
    column_scale = jnp.broadcast_to(column_scale, (NODES // BLK, BLK, TPB, BLK)).reshape(NODES, TPB, BLK)
    node_place = (jnp.arange(NODES, dtype=jnp.int32) % BLK)[:, None, None]
    tile_index = jnp.arange(TPB, dtype=jnp.int32)[None, :, None]
    column = jnp.arange(BLK, dtype=jnp.int32)[None, None, :]
    forced = (tile_index == 0) & (column == node_place)
    entries = jnp.where((chance < density) | forced, strength * column_scale, 0.0)
    return entries.astype(jnp.bfloat16)


def shard_levels(stream_key, extent, shards, low, largest):
    def one(position, shards_of):
        draws = jax.random.uniform(jax.random.fold_in(jax.random.fold_in(stream_key, 6), position), (shards_of,), jnp.float32, low / len(shards), largest / len(shards))
        return jnp.repeat(jnp.exp(draws), extent[position] // shards_of).reshape((-1,) + (1,) * (len(extent) - position - 1))

    factor_of = one(*shards[0])
    for cut in shards[1:]:
        factor_of = factor_of * one(*cut)
    return factor_of


def centred(stream_key, dims, scale, reach, cuts=(), kind=jnp.bfloat16):
    factor_of = shard_levels(stream_key, dims, cuts, -0.22, 0.18) if cuts else 1.0
    result = jax.random.normal(stream_key, dims, jnp.float32) * scale * factor_of
    return jnp.minimum(jnp.maximum(result, -reach), reach).astype(kind)


def setup_inputs(seed: int = 0) -> dict:
    streams_of = jax.random.split(jax.random.key(seed), 14)
    features = centred(streams_of[0], (NODES, F), 1.0, 6.0, ((0, 128),))
    history = centred(streams_of[1], (NODES, H), 1.0, 6.0, ((0, 128),))
    cotangent = centred(streams_of[2], (NODES, H), (NODES ** -0.5), 0.03125, ((0, 128),))
    adjacency = draw_adjacency(jax.random.fold_in(streams_of[13], 71), 0)
    tile_source = draw_tile_source(jax.random.fold_in(streams_of[13], 71), 0)
    col_sends = draw_col_sends(jax.random.fold_in(streams_of[13], 71), 0)
    col_counts = draw_col_counts(jax.random.fold_in(streams_of[13], 71), 0)
    row_sends = draw_row_sends(jax.random.fold_in(streams_of[13], 71), 0)
    row_counts = draw_row_counts(jax.random.fold_in(streams_of[13], 71), 0)
    first_self = centred(streams_of[9], (F, H), F ** -0.5, 0.25)
    first_neigh = centred(streams_of[10], (F, H), (F // 16) ** -0.5, 1.0)
    second_self = centred(streams_of[11], (H, H), H ** -0.5, 0.25)
    second_neigh = centred(streams_of[12], (H, H), (H // 16) ** -0.5, 1.0)
    return {"features": features, "history": history, "cotangent": cotangent, "adjacency": adjacency, "tile_source": tile_source, "col_sends": col_sends, "col_counts": col_counts, "row_sends": row_sends, "row_counts": row_counts, "first_self": first_self, "first_neigh": first_neigh, "second_self": second_self, "second_neigh": second_neigh}


def activation(inputs):
    return jax.nn.gelu(inputs, approximate=True)

def halo_maps(col_sends, col_counts, row_sends, row_counts):
    reader = jnp.arange(N_ROW * N_COL, dtype=jnp.int32)
    grid_row = (reader // N_COL)[:, None]
    grid_col = (reader % N_COL)[:, None]
    col_slot = jnp.arange(N_COL * CAP, dtype=jnp.int32)[None, :]
    col_owner = grid_row * N_COL + col_slot // CAP
    col_index = jnp.broadcast_to(col_slot % CAP, col_owner.shape)
    col_block = col_sends[col_owner, jnp.broadcast_to(grid_col, col_owner.shape), col_index]
    col_usable = col_index < col_counts[col_owner, jnp.broadcast_to(grid_col, col_owner.shape)]
    row_slot = jnp.arange(N_ROW * CAP, dtype=jnp.int32)[None, :]
    row_owner = row_slot // CAP * N_COL + grid_col
    row_index = jnp.broadcast_to(row_slot % CAP, row_owner.shape)
    row_block = row_sends[row_owner, jnp.broadcast_to(grid_row, row_owner.shape), row_index]
    row_usable = row_index < row_counts[row_owner, jnp.broadcast_to(grid_row, row_owner.shape)]
    owners = jnp.concatenate([col_owner, row_owner], axis=1)
    block_ids = jnp.concatenate([col_block, row_block], axis=1)
    usable = jnp.concatenate([col_usable, row_usable], axis=1)
    return (owners, block_ids, usable)

def take_halo(blocks_all, owners, block_ids, usable):
    picked = blocks_all[owners, block_ids]
    return jnp.where(usable[:, None, None], picked, jnp.zeros((), picked.dtype))

def aggregate(own_part, halo_part, adj_part, source_part):
    sources = jnp.concatenate([own_part, halo_part], axis=0)
    gathered = sources[source_part]
    adj_tiles = adj_part.reshape(NB, BLK, TPB, BLK)
    summed = jnp.einsum('irtc,itcw->irw', adj_tiles.astype(jnp.float32), gathered.astype(jnp.float32))
    return summed.reshape(NB * BLK, -1)

def reference(features, history, cotangent, adjacency, tile_source, col_sends, col_counts, row_sends, row_counts, first_self, first_neigh, second_self, second_neigh):
    partitions = N_ROW * N_COL
    owners, block_ids, usable = halo_maps(col_sends, col_counts, row_sends, row_counts)
    feat_all = features.reshape(partitions, NB, BLK, F)
    hist_all = history.reshape(partitions, NB, BLK, H)
    adj_all = adjacency.reshape(partitions, LOC, TPB, BLK)
    source_all = tile_source.reshape(partitions, NB, TPB)
    degree_all = lax.optimization_barrier(jnp.sum(adjacency.astype(jnp.float32), axis=(1, 2))).reshape(partitions, LOC, 1)
    cot_all = cotangent.reshape(partitions, LOC, H)

    def first_layer(partition):
        halo_part = take_halo(feat_all, owners[partition], block_ids[partition], usable[partition])
        summed = aggregate(feat_all[partition], halo_part, adj_all[partition], source_all[partition])
        first_mean = (summed / degree_all[partition]).astype(jnp.bfloat16)
        own_features = feat_all[partition].reshape(LOC, F)
        first_pre = jnp.dot(own_features, first_self, preferred_element_type=jnp.float32) + jnp.dot(first_mean, first_neigh, preferred_element_type=jnp.float32)
        return (first_mean, first_pre)

    def hidden_of(partition):
        return activation(first_layer(partition)[1]).astype(jnp.bfloat16)
    indices = jnp.arange(partitions, dtype=jnp.int32)
    hidden_all = lax.map(hidden_of, indices)
    hidden_blocks_all = hidden_all.reshape(partitions, NB, BLK, H)

    def second_step(totals, partition):
        first_mean, first_pre = first_layer(partition)
        first_hidden = hidden_all[partition]
        degree = degree_all[partition]
        hist_halo = take_halo(hist_all, owners[partition], block_ids[partition], usable[partition])
        summed = aggregate(hidden_blocks_all[partition], hist_halo, adj_all[partition], source_all[partition])
        second_mean = (summed / degree).astype(jnp.bfloat16)
        embed_part = (jnp.dot(first_hidden, second_self, preferred_element_type=jnp.float32) + jnp.dot(second_mean, second_neigh, preferred_element_type=jnp.float32)).astype(jnp.bfloat16)
        fresh_part = take_halo(hidden_blocks_all, owners[partition], block_ids[partition], usable[partition]).reshape(NH * BLK, H)
        upstream = cot_all[partition]
        grad_two_self = jnp.dot(first_hidden.T, upstream, preferred_element_type=jnp.float32)
        grad_two_neigh = jnp.dot(second_mean.T, upstream, preferred_element_type=jnp.float32)
        back_self = jnp.dot(upstream, second_self.T, preferred_element_type=jnp.float32)
        back_mean = (jnp.dot(upstream, second_neigh.T, preferred_element_type=jnp.float32) / degree).astype(jnp.bfloat16)
        adj_tiles = adj_all[partition].reshape(NB, BLK, TPB, BLK)
        spread = jnp.einsum('irtc,irw->itcw', adj_tiles.astype(jnp.float32), back_mean.reshape(NB, BLK, H).astype(jnp.float32))
        back_neigh = jax.ops.segment_sum(spread.reshape(NB * TPB, BLK, H), source_all[partition].reshape(-1), num_segments=NB + NH)[:NB].reshape(LOC, H)
        dummy, pullback = jax.vjp(activation, first_pre)
        back_pre = pullback(back_self + back_neigh)[0].astype(jnp.bfloat16)
        own_features = feat_all[partition].reshape(LOC, F)
        grad_one_self = jnp.dot(own_features.T, back_pre, preferred_element_type=jnp.float32)
        grad_one_neigh = jnp.dot(first_mean.T, back_pre, preferred_element_type=jnp.float32)
        totals = (totals[0] + grad_one_self, totals[1] + grad_one_neigh, totals[2] + grad_two_self, totals[3] + grad_two_neigh)
        return (totals, (embed_part, fresh_part))
    start = (jnp.zeros((F, H), jnp.float32), jnp.zeros((F, H), jnp.float32), jnp.zeros((H, H), jnp.float32), jnp.zeros((H, H), jnp.float32))
    totals, stacked = lax.scan(second_step, start, indices)
    embeddings = stacked[0].reshape(NODES, H)
    fresh_halo = stacked[1].reshape(HALO_ROWS, H)
    return (embeddings, fresh_halo, totals[0], totals[1], totals[2], totals[3])
```

```python
import functools

import jax
import jax.numpy as jnp
from jax import lax
from jax.experimental import pallas as pl
from jax.experimental.pallas import tpu as pltpu
from jax.sharding import PartitionSpec as P

MESH = pl.DeviceIdType.MESH
BF = jnp.bfloat16
F32 = jnp.float32
BLK = 128
TPB = 8
NB = 16
W = 512
LOC = NB * BLK
GELU_C = 0.7978845608028654
GELU_A = 0.044715

COL_OFFS = [
    (2, 2), (3, 2), (2, 3), (1, 2), (2, 1), (3, 1), (1, 3), (3, 3), (1, 1),
    (0, 2), (2, 0), (0, 3), (3, 0), (0, 1), (1, 0),
]
ROW_OFFS = [(2, 1), (2, 0), (3, 1), (1, 1), (3, 0), (1, 0), (0, 1)]
N_OFF = len(COL_OFFS) + len(ROW_OFFS)
TURNS = []
for _n in range(len(COL_OFFS)):
    TURNS.append(("col", _n))
    if _n % 2 == 0 and _n // 2 < len(ROW_OFFS):
        TURNS.append(("row", _n // 2))
FRESH_CUTS = (0, 22, 22, 22)


def dot(a, b):
    return jnp.dot(a, b, preferred_element_type=F32)


def dot_nt(a, b):
    return lax.dot_general(a, b, (((1,), (1,)), ((), ())), preferred_element_type=F32)


def dot_tn(a, b):
    return lax.dot_general(a, b, (((0,), (0,)), ((), ())), preferred_element_type=F32)


def blk(i):
    return pl.ds(pl.multiple_of(i * BLK, BLK), BLK)


def rows(i, n):
    return pl.ds(pl.multiple_of(i, n), n)


def kernel(
    feat_h, hist_h, cot_h, adj_h, ts, cs, cc, rs, rc, w1s_h, w1n_h, w2s_h, w2n_h,
    emb_h, fresh_h, grad_h,
    tab1, tab2, feat_v, hid_v, hist_v, snd_a, snd_b, cot, adjr, adjd, scr, deg, wts, fm, bm, acc, bp, sm, strip,
    rv1, s2, rv2, s3, h3, rv3, gfin,
    ld_sem, out_sem, a_ss, a_rs, b_ss, b_rs, f_ss, f_rs, r_ss, r_rs,
):
    c = lax.axis_index("col")
    r = lax.axis_index("row")
    x, y, z, k = c // 4, c % 4, r // 2, r % 2

    loads = [
        pltpu.make_async_copy(src, dst, ld_sem.at[n])
        for n, (src, dst) in enumerate(
            [
                (feat_h, feat_v),
                (hist_h, hist_v),
                (adj_h, adjr),
                (cot_h, cot),
                (w2s_h, wts.at[2]),
                (w2n_h, wts.at[3]),
                (w1s_h, wts.at[0]),
                (w1n_h, wts.at[1]),
                (feat_h, tab1.at[pl.ds(0, LOC)]),
            ]
        )
    ]
    for one in loads:
        one.start()

    def col_of(n, sign=1):
        a, b = COL_OFFS[n]
        dx = (1 - k) * a + k * b
        dy = (1 - k) * b + k * a
        return ((x + 4 + sign * dx) % 4) * 4 + (y + 4 + sign * dy) % 4

    def row_of(n, sign=1):
        a, b = ROW_OFFS[n]
        return ((z + 4 + sign * a) % 4) * 2 + (k + b) % 2

    barrier = pltpu.get_barrier_semaphore()
    for n in range(len(COL_OFFS)):
        pl.semaphore_signal(barrier, 1, device_id={"col": col_of(n)}, device_id_type=MESH)
    for n in range(len(ROW_OFFS)):
        pl.semaphore_signal(barrier, 1, device_id={"row": row_of(n)}, device_id_type=MESH)
    pl.semaphore_wait(barrier, N_OFF)

    def exchange(own, snd, dst, base, ssem, rsem, masked, first, last):
        copies = []
        for turn in range(first, last):
            kind, n = TURNS[turn]
            if kind == "col":
                to = col_of(n)
                which, live = cs[0, to, 0], cc[0, to]
                slot, device = base + c, {"col": to}
            else:
                to = row_of(n)
                which, live = rs[0, to, 0], rc[0, to]
                slot, device = base + 16 + r, {"row": to}
            chosen = own[pl.ds(which * BLK, BLK), :]
            if masked:
                chosen = jnp.where(jnp.full(chosen.shape, live, jnp.int32) > 0, chosen.astype(F32), 0.0)
                chosen = chosen.astype(BF)
            snd[pl.ds(turn * BLK, BLK), :] = chosen
            one = pltpu.make_async_remote_copy(
                src_ref=snd.at[pl.ds(turn * BLK, BLK)],
                dst_ref=dst.at[blk(slot)],
                send_sem=ssem.at[turn],
                recv_sem=rsem.at[turn],
                device_id=device,
                device_id_type=MESH,
            )
            one.start()
            copies.append(one)
        return copies

    loads[0].wait()
    feat_copies = exchange(feat_v, snd_a, tab1, NB, a_ss, a_rs, False, 0, N_OFF)
    loads[1].wait()
    hist_copies = exchange(hist_v, snd_b, tab2, NB, b_ss, b_rs, False, 0, N_OFF)

    zero_block = jnp.zeros((BLK, W), BF)
    for table in (tab1, tab2):
        table[blk(NB + c), :] = zero_block
        table[blk(NB + 16 + r), :] = zero_block

    loads[2].wait()

    @pl.loop(0, NB)
    def _(i):
        scr[...] = adjr[rows(i * BLK * TPB, BLK * TPB), :].astype(F32)
        total = jnp.zeros((BLK, BLK), F32)
        for t in range(TPB):
            tile = scr[pl.ds(t, BLK, stride=TPB), :]
            adjd[blk(i), pl.ds(t * BLK, BLK)] = tile.astype(BF)
            total += tile
        deg[blk(i), :] = jnp.broadcast_to(jnp.sum(total, axis=1, keepdims=True), (BLK, BLK))

    def divide(v, at):
        d = deg[at, :]
        return v / jnp.concatenate([d] * (W // BLK), axis=1)

    for n in range(3, 9):
        loads[n].wait()

    @pl.loop(0, 8)
    def _(m):
        at = rows(m * 256, 256)
        up = cot[at, :]
        acc[m // 2, rows((m % 2) * 256, 256), :] = dot_nt(up, wts[2])
        bm[at, :] = divide(dot_nt(up, wts[3]), at).astype(BF)

    @pl.loop(0, 8)
    def _(jp):
        @pl.loop(0, NB)
        def _(i):
            for jj in range(2):
                strip_part = jnp.zeros((BLK, BLK), F32)
                for t in range(TPB):
                    source = jnp.full((BLK, BLK), ts[i, t], jnp.int32)
                    tile = adjd[blk(i), pl.ds(t * BLK, BLK)].astype(F32)
                    strip_part += jnp.where(source == jp * 2 + jj, tile, 0.0)
                strip[blk(i), pl.ds(jj * BLK, BLK)] = strip_part.astype(BF)

        at = rows((jp % 2) * 256, 256)
        acc[jp // 2, at, :] += dot_tn(strip[...], bm[...])

    def aggregate(table, out):
        @pl.loop(0, NB)
        def _(i):
            total = jnp.zeros((BLK, W), F32)
            for t in range(0, TPB, 2):
                pair = jnp.concatenate(
                    [table[pl.ds(ts[i, t + d] * BLK, BLK), :] for d in range(2)], axis=0
                )
                total += dot(adjd[blk(i), pl.ds(t * BLK, 2 * BLK)], pair)
            out[blk(i), :] = divide(total, blk(i)).astype(BF)

    for one in feat_copies:
        one.wait_recv()
    aggregate(tab1, fm)

    @pl.loop(0, 8)
    def _(m):
        at = rows(m * 256, 256)
        v = dot(feat_v[at, :], wts[0]) + dot(fm[at, :], wts[1])
        t = jnp.tanh(GELU_C * (v + GELU_A * (v * v * v)))
        half = 0.5 * (1.0 + t)
        hidden = (v * half).astype(BF)
        hid_v[at, :] = hidden
        tab2[at, :] = hidden
        slope = half + 0.5 * v * (1.0 - t * t) * (GELU_C * (1.0 + 3.0 * GELU_A * (v * v)))
        bp[at, :] = (acc[m // 2, rows((m % 2) * 256, 256), :] * slope).astype(BF)

    for one in feat_copies:
        one.wait_send()
    fresh_copies = []

    def send_fresh(part):
        fresh_copies.extend(
            exchange(hid_v, snd_a, fresh_h, 0, f_ss, f_rs, True, FRESH_CUTS[part], FRESH_CUTS[part + 1])
        )

    send_fresh(0)

    def grad_of(g, left, right):
        @pl.loop(0, 4)
        def _(q):
            at = rows(q * BLK, BLK)
            acc[g, at, :] = dot_tn(left[:, at], right[...])

    grad_of(0, feat_v, bp)
    grad_of(1, fm, bp)
    grad_of(2, hid_v, cot)

    sems = iter(range(64))

    def send(src, dst, device):
        n = next(sems)
        one = pltpu.make_async_remote_copy(
            src_ref=src, dst_ref=dst, send_sem=r_ss.at[n], recv_sem=r_rs.at[n],
            device_id=device, device_id_type=MESH,
        )
        one.start()
        return one

    other = z * 2 + 1 - k
    reduce_copies = []

    def core_send(g, n):
        part = pl.ds(g, n)
        one = send(acc.at[part, rows((1 - k) * 256, 256)], rv1.at[part], {"row": other})
        reduce_copies.append(one)
        return one

    def z_send(g, n, core_copy):
        core_copy.wait_recv()
        for p in range(g, g + n):
            at = rows(k * 256, 256)
            both = acc[p, at, :] + rv1[p]
            acc[p, at, :] = both
            s2[p] = both.astype(BF)
        part = pl.ds(g, n)
        copies = []
        for d in range(3):
            zt = (z + d + 1) % 4
            copies.append(
                send(s2.at[part, rows(zt * 64, 64)], rv2.at[d, part], {"row": zt * 2 + k})
            )
        reduce_copies.extend(copies)
        return copies

    core_a = core_send(0, 3)
    for one in hist_copies:
        one.wait_recv()
    z_a = z_send(0, 3, core_a)
    send_fresh(1)
    aggregate(tab2, sm)
    grad_of(3, sm, cot)
    core_b = core_send(3, 1)

    snd_b_done = [one.wait_send() for one in hist_copies]
    snd_b[pl.ds(0, BLK), :] = zero_block
    own_slots = [
        pltpu.make_async_copy(snd_b.at[pl.ds(0, BLK)], fresh_h.at[blk(c)], out_sem.at[0]),
        pltpu.make_async_copy(snd_b.at[pl.ds(0, BLK)], fresh_h.at[blk(16 + r)], out_sem.at[1]),
    ]
    for one in own_slots:
        one.start()

    z_b = z_send(3, 1, core_b)

    @pl.loop(0, 4)
    def _(m):
        at = rows(m * 512, 512)
        bm[at, :] = (dot(hid_v[at, :], wts[2]) + dot(sm[at, :], wts[3])).astype(BF)

    emb_copy = pltpu.make_async_copy(bm, emb_h, out_sem.at[2])
    emb_copy.start()

    for one in z_a + z_b:
        one.wait_recv()
    for p in range(4):
        total = acc[p, rows(k * 256 + z * 64, 64), :]
        for d in range(3):
            total = total + rv2[d, p].astype(F32)
        h3[p] = total
        s3[p] = total.astype(BF)

    def piece(to):
        return (slice(None), rows((to // 4) * 16, 16), rows((to % 4) * BLK, BLK))

    xy_copies = []
    for n in range(len(COL_OFFS)):
        to = col_of(n)
        xy_copies.append(send(s3.at[piece(to)], rv3.at[n], {"col": to}))
    reduce_copies.extend(xy_copies)
    send_fresh(2)
    mine = (slice(None), rows(x * 16, 16), rows(y * BLK, BLK))
    final = h3[mine]
    for one in xy_copies:
        one.wait_recv()
    for n in range(len(COL_OFFS)):
        final = final + rv3[n].astype(F32)
    here = (slice(None), rows(k * 256 + z * 64 + x * 16, 16), rows(y * BLK, BLK))
    gfin[here] = final.astype(BF)

    gather = [send(gfin.at[here], gfin.at[here], {"col": col_of(n)}) for n in range(len(COL_OFFS))]
    for one in gather:
        one.wait_recv()
    reduce_copies.extend(gather)
    strip_z = (slice(None), rows(k * 256 + z * 64, 64))
    gather = [send(gfin.at[strip_z], gfin.at[strip_z], {"row": ((z + d + 1) % 4) * 2 + k}) for d in range(3)]
    for one in gather:
        one.wait_recv()
    reduce_copies.extend(gather)
    strip_k = (slice(None), rows(k * 256, 256))
    one = send(gfin.at[strip_k], gfin.at[strip_k], {"row": other})
    one.wait_recv()
    reduce_copies.append(one)
    grad_copy = pltpu.make_async_copy(gfin, grad_h, out_sem.at[3])
    grad_copy.start()

    for one in fresh_copies:
        one.wait_recv()
    for one in fresh_copies + reduce_copies:
        one.wait_send()
    for one in own_slots:
        one.wait()
    emb_copy.wait()
    grad_copy.wait()


def body(
    features, history, cotangent, adjacency, tile_source, col_sends, col_counts, row_sends, row_counts,
    first_self, first_neigh, second_self, second_neigh,
):
    anyspace = pl.BlockSpec(memory_space=pl.ANY)
    smem = pl.BlockSpec(memory_space=pltpu.SMEM)
    vm = pltpu.VMEM
    dma = pltpu.SemaphoreType.DMA
    emb, fresh, grads = pl.pallas_call(
        kernel,
        out_shape=(
            jax.ShapeDtypeStruct((LOC, W), BF),
            jax.ShapeDtypeStruct((24 * BLK, W), BF),
            jax.ShapeDtypeStruct((4, W, W), BF),
        ),
        in_specs=[anyspace] * 4 + [smem] * 5 + [anyspace] * 4,
        out_specs=(anyspace,) * 3,
        scratch_shapes=[
            vm((40 * BLK, W), BF),
            vm((40 * BLK, W), BF),
            vm((LOC, W), BF),
            vm((LOC, W), BF),
            vm((LOC, W), BF),
            vm((N_OFF * BLK, W), BF),
            vm((N_OFF * BLK, W), BF),
            vm((LOC, W), BF),
            vm((LOC * TPB, BLK), BF),
            vm((LOC, TPB * BLK), BF),
            vm((BLK * TPB, BLK), F32),
            vm((LOC, BLK), F32),
            vm((4, W, W), BF),
            vm((LOC, W), BF),
            vm((LOC, W), BF),
            vm((4, W, W), F32),
            vm((LOC, W), BF),
            vm((LOC, W), BF),
            vm((LOC, 2 * BLK), BF),
            vm((4, 256, W), F32),
            vm((4, 256, W), BF),
            vm((3, 4, 64, W), BF),
            vm((4, 64, W), BF),
            vm((4, 64, W), F32),
            vm((15, 4, 16, BLK), BF),
            vm((4, W, W), BF),
            dma((9,)), dma((4,)),
            dma((N_OFF,)), dma((N_OFF,)), dma((N_OFF,)), dma((N_OFF,)), dma((N_OFF,)), dma((N_OFF,)),
            dma((42,)), dma((42,)),
        ],
        compiler_params=pltpu.CompilerParams(
            collective_id=0, has_side_effects=True, vmem_limit_bytes=61 * 2**20
        ),
        cost_estimate=pl.CostEstimate(flops=18 * 10**9, bytes_accessed=24 * 2**20, transcendentals=2**20),
    )(
        features, history, cotangent, adjacency.reshape(LOC * TPB, BLK), tile_source,
        col_sends, col_counts, row_sends, row_counts,
        first_self, first_neigh, second_self, second_neigh,
    )
    return emb, fresh, *(grads[n].astype(F32) for n in range(4))


def solution(mesh):
    nodes = P(("row", "col"), None)
    cube = P(("row", "col"), None, None)
    placed = (nodes, nodes, nodes, cube, nodes, cube, nodes, cube, nodes, P(), P(), P(), P())
    return jax.shard_map(
        body, mesh=mesh, in_specs=placed,
        out_specs=(nodes, nodes, P(), P(), P(), P()), check_vma=False,
    )
```

```python
import functools

import jax
import jax.numpy as jnp
from jax import lax
from jax.experimental import pallas as pl
from jax.experimental.pallas import tpu as pltpu
from jax.sharding import PartitionSpec as P

MESH = pl.DeviceIdType.MESH
BF = jnp.bfloat16
F32 = jnp.float32
BLK = 128
TPB = 8
NB = 16
W = 512
LOC = NB * BLK
RING = 4
ROWS_EARLY = 4
GELU_C = 0.7978845608028654
GELU_A = 0.044715

COL_OFFS = [
    (2, 2), (3, 2), (2, 3), (1, 2), (2, 1), (3, 1), (1, 3), (3, 3), (1, 1),
    (0, 2), (2, 0), (0, 3), (3, 0), (0, 1), (1, 0),
]
ROW_OFFS = [(2, 1), (2, 0), (3, 1), (1, 1), (3, 0), (1, 0), (0, 1)]
N_OFF = len(COL_OFFS) + len(ROW_OFFS)
TURNS = []
for _n in range(len(COL_OFFS)):
    TURNS.append(("col", _n))
    if _n % 2 == 0 and _n // 2 < len(ROW_OFFS):
        TURNS.append(("row", _n // 2))
FRESH_CUTS = (0, 5, 8, 11, 13, 15)


def dot(a, b):
    return jnp.dot(a, b, preferred_element_type=F32)


def dot_nt(a, b):
    return lax.dot_general(a, b, (((1,), (1,)), ((), ())), preferred_element_type=F32)


def dot_tn(a, b):
    return lax.dot_general(a, b, (((0,), (0,)), ((), ())), preferred_element_type=F32)


def blk(i):
    return pl.ds(pl.multiple_of(i * BLK, BLK), BLK)


def rows(i, n):
    return pl.ds(pl.multiple_of(i, n), n)


def kernel(
    feat_h, hist_h, cot_h, adj_h, ts, cs, cc, rs, rc, w1s_h, w1n_h, w2s_h, w2n_h,
    emb_h, fresh_h, grad_h,
    tab1, tab2, feat_v, hid_v, hist_v, snd_a, snd_b, cot, adjr, adjd, scr, deg, wts, fm, bm, acc, strip,
    rv1, s2, rv2, s3, h3, rv3, g3, gfin,
    ld_sem, adj_sem, out_sem, a_ss, a_rs, b_ss, b_rs, f_ss, f_rs, r_ss, r_rs,
):
    bp, sm = hist_v, fm
    c = lax.axis_index("col")
    r = lax.axis_index("row")
    x, y, z, k = c // 4, c % 4, r // 2, r % 2

    loads = [
        pltpu.make_async_copy(src, dst, ld_sem.at[n])
        for n, (src, dst) in enumerate(
            [
                (feat_h, feat_v),
                (hist_h, hist_v),
                (cot_h, cot),
                (w2s_h, wts.at[2]),
                (w2n_h, wts.at[3]),
                (w1s_h, wts.at[0]),
                (w1n_h, wts.at[1]),
                (feat_h, tab1.at[pl.ds(0, LOC)]),
            ]
        )
    ]
    for one in loads:
        one.start()

    def col_of(n, sign=1):
        a, b = COL_OFFS[n]
        dx = (1 - k) * a + k * b
        dy = (1 - k) * b + k * a
        return ((x + 4 + sign * dx) % 4) * 4 + (y + 4 + sign * dy) % 4

    def row_of(n, sign=1):
        a, b = ROW_OFFS[n]
        return ((z + 4 + sign * a) % 4) * 2 + (k + b) % 2

    barrier = pltpu.get_barrier_semaphore()
    for n in range(len(COL_OFFS)):
        pl.semaphore_signal(barrier, 1, device_id={"col": col_of(n)}, device_id_type=MESH)
    for n in range(len(ROW_OFFS)):
        pl.semaphore_signal(barrier, 1, device_id={"row": row_of(n)}, device_id_type=MESH)
    pl.semaphore_wait(barrier, N_OFF)

    def exchange(own, snd, dst, base, ssem, rsem, masked, turns):
        copies = []
        for kind, n in turns:
            turn = n if kind == "col" else len(COL_OFFS) + n
            if kind == "col":
                to = col_of(n)
                which, live = cs[0, to], cc[0, to]
                slot, device = base + c, {"col": to}
            else:
                to = row_of(n)
                which, live = rs[0, to], rc[0, to]
                slot, device = base + 16 + r, {"row": to}
            chosen = own[pl.ds(which * BLK, BLK), :]
            if masked:
                chosen = jnp.where(jnp.full(chosen.shape, live, jnp.int32) > 0, chosen.astype(F32), 0.0)
                chosen = chosen.astype(BF)
            snd[pl.ds(turn * BLK, BLK), :] = chosen
            one = pltpu.make_async_remote_copy(
                src_ref=snd.at[pl.ds(turn * BLK, BLK)],
                dst_ref=dst.at[blk(slot)],
                send_sem=ssem.at[turn],
                recv_sem=rsem.at[turn],
                device_id=device,
                device_id_type=MESH,
            )
            one.start()
            copies.append(one)
        return copies

    loads[0].wait()
    feat_copies = exchange(feat_v, snd_a, tab1, NB, a_ss, a_rs, False, TURNS)
    loads[1].wait()
    hist_copies = exchange(hist_v, snd_b, tab2, NB, b_ss, b_rs, False, TURNS)

    zero_block = jnp.zeros((BLK, W), BF)
    for table in (tab1, tab2):
        table[blk(NB + c), :] = zero_block
        table[blk(NB + 16 + r), :] = zero_block


    def adj_load(i):
        return pltpu.make_async_copy(
            adj_h.at[rows(i * BLK * TPB, BLK * TPB)], adjr.at[i % RING], adj_sem.at[i % RING]
        )

    for i in range(RING):
        adj_load(i).start()

    @pl.loop(0, NB)
    def _(i):
        adj_load(i).wait()
        scr[...] = adjr[i % RING].astype(F32)

        @pl.when(i + RING < NB)
        def _():
            adj_load(i + RING).start()

        total = jnp.zeros((BLK, BLK), F32)
        for t in range(TPB):
            tile = scr[pl.ds(t, BLK, stride=TPB), :]
            adjd[blk(i), pl.ds(t * BLK, BLK)] = tile.astype(BF)
            total += tile
        deg[blk(i), :] = jnp.broadcast_to(jnp.sum(total, axis=1, keepdims=True), (BLK, BLK))

    def divide(v, at):
        d = deg[at, :]
        return v / jnp.concatenate([d] * (W // BLK), axis=1)

    for n in range(2, 8):
        loads[n].wait()

    @pl.loop(0, 8)
    def _(m):
        at = rows(m * 256, 256)
        up = cot[at, :]
        acc[m // 2, rows((m % 2) * 256, 256), :] = dot_nt(up, wts[2])
        bm[at, :] = divide(dot_nt(up, wts[3]), at).astype(BF)

    @pl.loop(0, 8)
    def _(jp):
        @pl.loop(0, NB)
        def _(i):
            for jj in range(2):
                strip_part = jnp.zeros((BLK, BLK), BF)
                for t in range(TPB):
                    source = jnp.full((BLK, BLK), ts[t, i], jnp.int32)
                    hit = jnp.where(source == jp * 2 + jj, 1.0, 0.0).astype(BF)
                    strip_part += hit * adjd[blk(i), pl.ds(t * BLK, BLK)]
                strip[blk(i), pl.ds(jj * BLK, BLK)] = strip_part

        at = rows((jp % 2) * 256, 256)
        acc[jp // 2, at, :] += dot_tn(strip[...], bm[...])

    def aggregate(table, out):
        @pl.loop(0, NB)
        def _(i):
            total = jnp.zeros((BLK, W), F32)
            for t in range(0, TPB, 2):
                pair = jnp.concatenate(
                    [table[pl.ds(ts[t + d, i] * BLK, BLK), :] for d in range(2)], axis=0
                )
                total += dot(adjd[blk(i), pl.ds(t * BLK, 2 * BLK)], pair)
            out[blk(i), :] = divide(total, blk(i)).astype(BF)

    for one in feat_copies:
        one.wait_recv()
    aggregate(tab1, fm)

    @pl.loop(0, 8)
    def _(m):
        at = rows(m * 256, 256)
        v = dot(feat_v[at, :], wts[0]) + dot(fm[at, :], wts[1])
        t = jnp.tanh(GELU_C * (v + GELU_A * (v * v * v)))
        half = 0.5 * (1.0 + t)
        hidden = (v * half).astype(BF)
        hid_v[at, :] = hidden
        tab2[at, :] = hidden
        slope = half + 0.5 * v * (1.0 - t * t) * (GELU_C * (1.0 + 3.0 * GELU_A * (v * v)))
        bp[at, :] = (acc[m // 2, rows((m % 2) * 256, 256), :] * slope).astype(BF)

    for one in feat_copies:
        one.wait_send()
    fresh_copies = []

    def send_fresh(turns):
        fresh_copies.extend(exchange(hid_v, snd_a, fresh_h, 0, f_ss, f_rs, True, turns))

    def send_fresh_cols(part):
        send_fresh([("col", n) for n in range(FRESH_CUTS[part], FRESH_CUTS[part + 1])])

    send_fresh([("row", n) for n in range(ROWS_EARLY)])
    send_fresh_cols(0)

    def grad_of(g, left, right):
        @pl.loop(0, 4)
        def _(q):
            at = rows(q * BLK, BLK)
            acc[g, at, :] = dot_tn(left[:, at], right[...])

    sems = iter(range(96))
    other = z * 2 + 1 - k
    row_base = k * 256 + z * 64
    reduce_copies = []

    def send(src, dst, device):
        n = next(sems)
        one = pltpu.make_async_remote_copy(
            src_ref=src, dst_ref=dst, send_sem=r_ss.at[n], recv_sem=r_rs.at[n],
            device_id=device, device_id_type=MESH,
        )
        one.start()
        reduce_copies.append(one)
        return one

    def arrived(copies):
        for one in copies:
            one.wait_recv()

    def core_send(g, n):
        part = pl.ds(g, n)
        return [send(acc.at[part, rows((1 - k) * 256, 256)], rv1.at[part], {"row": other})]

    def z_send(g, n):
        for p in range(g, g + n):
            at = rows(k * 256, 256)
            both = acc[p, at, :] + rv1[p]
            acc[p, at, :] = both
            s2[p] = both.astype(BF)
        part = pl.ds(g, n)
        copies = []
        for d in range(3):
            zt = (z + d + 1) % 4
            copies.append(send(s2.at[part, rows(zt * 64, 64)], rv2.at[d, part], {"row": zt * 2 + k}))
        return copies

    def xy_send(g, n):
        for p in range(g, g + n):
            total = acc[p, rows(row_base, 64), :]
            for d in range(3):
                total = total + rv2[d, p].astype(F32)
            for d in range(16):
                cut = total[(d // 4) * 16 : (d // 4) * 16 + 16, (d % 4) * BLK : (d % 4) * BLK + BLK]
                h3[d, pl.ds(p * 16, 16), :] = cut
                s3[d, pl.ds(p * 16, 16), :] = cut.astype(BF)
        part = pl.ds(g * 16, n * 16)
        copies = []
        for m in range(len(COL_OFFS)):
            to = col_of(m)
            copies.append(send(s3.at[to, part], rv3.at[m, part], {"col": to}))
        return copies

    def xy_gather(g, n):
        part = pl.ds(g * 16, n * 16)
        total = h3[c, part, :]
        for m in range(len(COL_OFFS)):
            total = total + rv3[m, part, :].astype(F32)
        g3[c, part, :] = total.astype(BF)
        here = g3.at[c, part]
        return [send(here, here, {"col": col_of(m)}) for m in range(len(COL_OFFS))]

    def z_gather(g, n):
        for p in range(g, g + n):
            for d in range(16):
                at = rows(row_base + (d // 4) * 16, 16)
                gfin[p, at, pl.ds((d % 4) * BLK, BLK)] = g3[d, pl.ds(p * 16, 16), :]
        here = gfin.at[pl.ds(g, n), rows(row_base, 64)]
        return [send(here, here, {"row": ((z + d + 1) % 4) * 2 + k}) for d in range(3)]

    def core_gather(g, n):
        here = gfin.at[pl.ds(g, n), rows(k * 256, 256)]
        return [send(here, here, {"row": other})]

    z_a = []
    grad_of(2, hid_v, cot)
    core_2 = core_send(2, 1)
    grad_of(0, feat_v, bp)
    core_0 = core_send(0, 1)
    arrived(core_2)
    z_a += z_send(2, 1)
    grad_of(1, fm, bp)
    core_1 = core_send(1, 1)
    arrived(core_0)
    z_a += z_send(0, 1)
    arrived(core_1)
    z_a += z_send(1, 1)
    send_fresh([("row", n) for n in range(ROWS_EARLY, len(ROW_OFFS))])

    arrived(hist_copies)
    aggregate(tab2, sm)
    arrived(z_a)
    xy_a = xy_send(0, 3)
    grad_of(3, sm, cot)
    core_b = core_send(3, 1)
    send_fresh_cols(1)

    for one in hist_copies:
        one.wait_send()
    snd_b[pl.ds(0, BLK), :] = zero_block
    own_slots = [
        pltpu.make_async_copy(snd_b.at[pl.ds(0, BLK)], fresh_h.at[blk(c)], out_sem.at[0]),
        pltpu.make_async_copy(snd_b.at[pl.ds(0, BLK)], fresh_h.at[blk(16 + r)], out_sem.at[1]),
    ]
    for one in own_slots:
        one.start()

    arrived(core_b)
    z_b = z_send(3, 1)
    arrived(xy_a)
    xy_a = xy_gather(0, 3)
    send_fresh_cols(2)

    @pl.loop(0, 4)
    def _(m):
        at = rows(m * 512, 512)
        bm[at, :] = (dot(hid_v[at, :], wts[2]) + dot(sm[at, :], wts[3])).astype(BF)

    emb_copy = pltpu.make_async_copy(bm, emb_h, out_sem.at[2])
    emb_copy.start()

    arrived(z_b)
    xy_b = xy_send(3, 1)
    send_fresh_cols(3)
    arrived(xy_a)
    z_a = z_gather(0, 3)
    arrived(xy_b)
    xy_b = xy_gather(3, 1)
    send_fresh_cols(4)
    arrived(xy_b)
    z_b = z_gather(3, 1)
    arrived(z_a)
    core_a = core_gather(0, 3)
    arrived(z_b)
    core_b = core_gather(3, 1)
    arrived(core_a + core_b)
    grad_copy = pltpu.make_async_copy(gfin, grad_h, out_sem.at[3])
    grad_copy.start()

    for one in fresh_copies:
        one.wait_recv()
    for one in fresh_copies + reduce_copies:
        one.wait_send()
    for one in own_slots:
        one.wait()
    emb_copy.wait()
    grad_copy.wait()


def body(
    features, history, cotangent, adjacency, tile_source, col_sends, col_counts, row_sends, row_counts,
    first_self, first_neigh, second_self, second_neigh,
):
    anyspace = pl.BlockSpec(memory_space=pl.ANY)
    smem = pl.BlockSpec(memory_space=pltpu.SMEM)
    vm = pltpu.VMEM
    dma = pltpu.SemaphoreType.DMA
    emb, fresh, grads = pl.pallas_call(
        kernel,
        out_shape=(
            jax.ShapeDtypeStruct((LOC, W), BF),
            jax.ShapeDtypeStruct((24 * BLK, W), BF),
            jax.ShapeDtypeStruct((4, W, W), BF),
        ),
        in_specs=[anyspace] * 4 + [smem] * 5 + [anyspace] * 4,
        out_specs=(anyspace,) * 3,
        scratch_shapes=[
            vm((40 * BLK, W), BF),
            vm((40 * BLK, W), BF),
            vm((LOC, W), BF),
            vm((LOC, W), BF),
            vm((LOC, W), BF),
            vm((N_OFF * BLK, W), BF),
            vm((N_OFF * BLK, W), BF),
            vm((LOC, W), BF),
            vm((RING, BLK * TPB, BLK), BF),
            vm((LOC, TPB * BLK), BF),
            vm((BLK * TPB, BLK), F32),
            vm((LOC, BLK), F32),
            vm((4, W, W), BF),
            vm((LOC, W), BF),
            vm((LOC, W), BF),
            vm((4, W, W), F32),
            vm((LOC, 2 * BLK), BF),
            vm((4, 256, W), F32),
            vm((4, 256, W), BF),
            vm((3, 4, 64, W), BF),
            vm((16, 64, BLK), BF),
            vm((16, 64, BLK), F32),
            vm((15, 64, BLK), BF),
            vm((16, 64, BLK), BF),
            vm((4, W, W), BF),
            dma((8,)), dma((RING,)), dma((4,)),
            dma((N_OFF,)), dma((N_OFF,)), dma((N_OFF,)), dma((N_OFF,)), dma((N_OFF,)), dma((N_OFF,)),
            dma((96,)), dma((96,)),
        ],
        compiler_params=pltpu.CompilerParams(
            collective_id=0, has_side_effects=True, vmem_limit_bytes=56 * 2**20
        ),
        cost_estimate=pl.CostEstimate(flops=18 * 10**9, bytes_accessed=24 * 2**20, transcendentals=2**20),
    )(
        features, history, cotangent, adjacency.reshape(LOC * TPB, BLK), tile_source.T,
        col_sends.reshape(1, -1), col_counts, row_sends.reshape(1, -1), row_counts,
        first_self, first_neigh, second_self, second_neigh,
    )
    return emb, fresh, *(grads[n].astype(F32) for n in range(4))


def solution(mesh):
    nodes = P(("row", "col"), None)
    cube = P(("row", "col"), None, None)
    placed = (nodes, nodes, nodes, cube, nodes, cube, nodes, cube, nodes, P(), P(), P(), P())
    return jax.shard_map(
        body, mesh=mesh, in_specs=placed,
        out_specs=(nodes, nodes, P(), P(), P(), P()), check_vma=False,
    )
```

```python
import functools

import jax
import jax.numpy as jnp
from jax import lax
from jax.experimental import pallas as pl
from jax.experimental.pallas import tpu as pltpu
from jax.sharding import PartitionSpec as P

MESH = pl.DeviceIdType.MESH
BF = jnp.bfloat16
F32 = jnp.float32
BLK = 128
TPB = 8
NB = 16
W = 512
LOC = NB * BLK
RING = 4
ROWS_EARLY = 4
GELU_C = 0.7978845608028654
GELU_A = 0.044715

COL_OFFS = [
    (2, 2), (3, 2), (2, 3), (1, 2), (2, 1), (3, 1), (1, 3), (3, 3), (1, 1),
    (0, 2), (2, 0), (0, 3), (3, 0), (0, 1), (1, 0),
]
ROW_OFFS = [(2, 1), (2, 0), (3, 1), (1, 1), (3, 0), (1, 0), (0, 1)]
N_OFF = len(COL_OFFS) + len(ROW_OFFS)
TURNS = []
for _n in range(len(COL_OFFS)):
    TURNS.append(("col", _n))
    if _n % 2 == 0 and _n // 2 < len(ROW_OFFS):
        TURNS.append(("row", _n // 2))
FRESH_CUTS = (0, 5, 8, 11, 13, 15)


def dot(a, b):
    return jnp.dot(a, b, preferred_element_type=F32)


def dot_nt(a, b):
    return lax.dot_general(a, b, (((1,), (1,)), ((), ())), preferred_element_type=F32)


def dot_tn(a, b):
    return lax.dot_general(a, b, (((0,), (0,)), ((), ())), preferred_element_type=F32)


def blk(i):
    return pl.ds(pl.multiple_of(i * BLK, BLK), BLK)


def rows(i, n):
    return pl.ds(pl.multiple_of(i, n), n)


def kernel(
    feat_h, hist_h, cot_h, adj_h, ts, cs, cc, rs, rc, w1s_h, w1n_h, w2s_h, w2n_h,
    emb_h, fresh_h, grad_h,
    tab1, tab2, feat_v, hid_v, hist_v, snd_a, snd_b, cot, adjr, adjd, scr, deg, wts, fm, bm, acc, strip,
    rv1, s2, rv2, s3, h3, rv3, g3, gfin,
    ld_sem, adj_sem, out_sem, a_ss, a_rs, b_ss, b_rs, f_ss, f_rs, r_ss, r_rs,
):
    bp, sm = hist_v, fm
    c = lax.axis_index("col")
    r = lax.axis_index("row")
    x, y, z, k = c // 4, c % 4, r // 2, r % 2

    loads = [
        pltpu.make_async_copy(src, dst, ld_sem.at[n])
        for n, (src, dst) in enumerate(
            [
                (feat_h, feat_v),
                (hist_h, hist_v),
                (cot_h, cot),
                (w2s_h, wts.at[2]),
                (w2n_h, wts.at[3]),
                (w1s_h, wts.at[0]),
                (w1n_h, wts.at[1]),
                (feat_h, tab1.at[pl.ds(0, LOC)]),
            ]
        )
    ]
    for one in loads:
        one.start()

    def col_of(n, sign=1):
        a, b = COL_OFFS[n]
        dx = (1 - k) * a + k * b
        dy = (1 - k) * b + k * a
        return ((x + 4 + sign * dx) % 4) * 4 + (y + 4 + sign * dy) % 4

    def row_of(n, sign=1):
        a, b = ROW_OFFS[n]
        return ((z + 4 + sign * a) % 4) * 2 + (k + b) % 2

    barrier = pltpu.get_barrier_semaphore()
    for n in range(len(COL_OFFS)):
        pl.semaphore_signal(barrier, 1, device_id={"col": col_of(n)}, device_id_type=MESH)
    for n in range(len(ROW_OFFS)):
        pl.semaphore_signal(barrier, 1, device_id={"row": row_of(n)}, device_id_type=MESH)
    pl.semaphore_wait(barrier, N_OFF)

    def exchange(own, snd, dst, base, ssem, rsem, masked, turns):
        copies = []
        for kind, n in turns:
            turn = n if kind == "col" else len(COL_OFFS) + n
            if kind == "col":
                to = col_of(n)
                which, live = cs[0, to], cc[0, to]
                slot, device = base + c, {"col": to}
            else:
                to = row_of(n)
                which, live = rs[0, to], rc[0, to]
                slot, device = base + 16 + r, {"row": to}
            chosen = own[pl.ds(which * BLK, BLK), :]
            if masked:
                chosen = jnp.where(jnp.full(chosen.shape, live, jnp.int32) > 0, chosen.astype(F32), 0.0)
                chosen = chosen.astype(BF)
            snd[pl.ds(turn * BLK, BLK), :] = chosen
            one = pltpu.make_async_remote_copy(
                src_ref=snd.at[pl.ds(turn * BLK, BLK)],
                dst_ref=dst.at[blk(slot)],
                send_sem=ssem.at[turn],
                recv_sem=rsem.at[turn],
                device_id=device,
                device_id_type=MESH,
            )
            one.start()
            copies.append(one)
        return copies

    loads[0].wait()
    feat_copies = exchange(feat_v, snd_a, tab1, NB, a_ss, a_rs, False, TURNS)
    loads[1].wait()
    hist_copies = exchange(hist_v, snd_b, tab2, NB, b_ss, b_rs, False, TURNS)

    zero_block = jnp.zeros((BLK, W), BF)
    for table in (tab1, tab2):
        table[blk(NB + c), :] = zero_block
        table[blk(NB + 16 + r), :] = zero_block


    def adj_load(i):
        return pltpu.make_async_copy(
            adj_h.at[rows(i * BLK * TPB, BLK * TPB)], adjr.at[i % RING], adj_sem.at[i % RING]
        )

    for i in range(RING):
        adj_load(i).start()

    @pl.loop(0, NB)
    def _(i):
        adj_load(i).wait()
        scr[...] = adjr[i % RING].astype(F32)

        @pl.when(i + RING < NB)
        def _():
            adj_load(i + RING).start()

        total = jnp.zeros((BLK, BLK), F32)
        for t in range(TPB):
            tile = scr[pl.ds(t, BLK, stride=TPB), :]
            adjd[blk(i), pl.ds(t * BLK, BLK)] = tile.astype(BF)
            total += tile
        deg[blk(i), :] = jnp.broadcast_to(jnp.sum(total, axis=1, keepdims=True), (BLK, BLK))

    def divide(v, at):
        d = deg[at, :]
        return v / jnp.concatenate([d] * (W // BLK), axis=1)

    for n in range(2, 8):
        loads[n].wait()

    @pl.loop(0, 8)
    def _(m):
        at = rows(m * 256, 256)
        up = cot[at, :]
        acc[m // 2, rows((m % 2) * 256, 256), :] = dot_nt(up, wts[2])
        bm[at, :] = divide(dot_nt(up, wts[3]), at).astype(BF)

    @pl.loop(0, 8)
    def _(jp):
        @pl.loop(0, NB)
        def _(i):
            for jj in range(2):
                strip_part = jnp.zeros((BLK, BLK), BF)
                for t in range(TPB):
                    source = jnp.full((BLK, BLK), ts[t, i], jnp.int32)
                    hit = jnp.where(source == jp * 2 + jj, 1.0, 0.0).astype(BF)
                    strip_part += hit * adjd[blk(i), pl.ds(t * BLK, BLK)]
                strip[blk(i), pl.ds(jj * BLK, BLK)] = strip_part

        at = rows((jp % 2) * 256, 256)
        acc[jp // 2, at, :] += dot_tn(strip[...], bm[...])

    def aggregate(table, out):
        @pl.loop(0, NB)
        def _(i):
            total = jnp.zeros((BLK, W), F32)
            for t in range(0, TPB, 2):
                pair = jnp.concatenate(
                    [table[pl.ds(ts[t + d, i] * BLK, BLK), :] for d in range(2)], axis=0
                )
                total += dot(adjd[blk(i), pl.ds(t * BLK, 2 * BLK)], pair)
            out[blk(i), :] = divide(total, blk(i)).astype(BF)

    for one in feat_copies:
        one.wait_recv()
    aggregate(tab1, fm)

    @pl.loop(0, 8)
    def _(m):
        at = rows(m * 256, 256)
        v = dot(feat_v[at, :], wts[0]) + dot(fm[at, :], wts[1])
        t = jnp.tanh(GELU_C * (v + GELU_A * (v * v * v)))
        half = 0.5 * (1.0 + t)
        hidden = (v * half).astype(BF)
        hid_v[at, :] = hidden
        tab2[at, :] = hidden
        slope = half + 0.5 * v * (1.0 - t * t) * (GELU_C * (1.0 + 3.0 * GELU_A * (v * v)))
        bp[at, :] = (acc[m // 2, rows((m % 2) * 256, 256), :] * slope).astype(BF)

    for one in feat_copies:
        one.wait_send()
    fresh_copies = []

    def send_fresh(turns):
        fresh_copies.extend(exchange(hid_v, snd_a, fresh_h, 0, f_ss, f_rs, True, turns))

    def send_fresh_cols(part):
        send_fresh([("col", n) for n in range(FRESH_CUTS[part], FRESH_CUTS[part + 1])])

    send_fresh([("row", n) for n in range(ROWS_EARLY)])
    send_fresh_cols(0)

    def grad_of(g, left, right):
        @pl.loop(0, 4)
        def _(q):
            at = rows(q * BLK, BLK)
            acc[g, at, :] = dot_tn(left[:, at], right[...])

    sems = iter(range(96))
    other = z * 2 + 1 - k
    row_base = k * 256 + z * 64
    reduce_copies = []

    def send(src, dst, device):
        n = next(sems)
        one = pltpu.make_async_remote_copy(
            src_ref=src, dst_ref=dst, send_sem=r_ss.at[n], recv_sem=r_rs.at[n],
            device_id=device, device_id_type=MESH,
        )
        one.start()
        reduce_copies.append(one)
        return one

    def arrived(copies):
        for one in copies:
            one.wait_recv()

    def core_send(g, n):
        part = pl.ds(g, n)
        return [send(acc.at[part, rows((1 - k) * 256, 256)], rv1.at[part], {"row": other})]

    def z_send(g, n):
        for p in range(g, g + n):
            at = rows(k * 256, 256)
            both = acc[p, at, :] + rv1[p]
            acc[p, at, :] = both
            s2[p] = both.astype(BF)
        part = pl.ds(g, n)
        copies = []
        for d in range(3):
            zt = (z + d + 1) % 4
            copies.append(send(s2.at[part, rows(zt * 64, 64)], rv2.at[d, part], {"row": zt * 2 + k}))
        return copies

    def xy_send(g, n):
        for p in range(g, g + n):
            total = acc[p, rows(row_base, 64), :]
            for d in range(3):
                total = total + rv2[d, p].astype(F32)
            for d in range(16):
                cut = total[(d // 4) * 16 : (d // 4) * 16 + 16, (d % 4) * BLK : (d % 4) * BLK + BLK]
                h3[d, pl.ds(p * 16, 16), :] = cut
                s3[d, pl.ds(p * 16, 16), :] = cut.astype(BF)
        part = pl.ds(g * 16, n * 16)
        copies = []
        for m in range(len(COL_OFFS)):
            to = col_of(m)
            copies.append(send(s3.at[to, part], rv3.at[m, part], {"col": to}))
        return copies

    def xy_gather(g, n):
        part = pl.ds(g * 16, n * 16)
        total = h3[c, part, :]
        for m in range(len(COL_OFFS)):
            total = total + rv3[m, part, :].astype(F32)
        g3[c, part, :] = total.astype(BF)
        here = g3.at[c, part]
        return [send(here, here, {"col": col_of(m)}) for m in range(len(COL_OFFS))]

    def z_gather(g, n):
        for p in range(g, g + n):
            for d in range(16):
                at = rows(row_base + (d // 4) * 16, 16)
                gfin[p, at, pl.ds((d % 4) * BLK, BLK)] = g3[d, pl.ds(p * 16, 16), :]
        here = gfin.at[pl.ds(g, n), rows(row_base, 64)]
        return [send(here, here, {"row": ((z + d + 1) % 4) * 2 + k}) for d in range(3)]

    def core_gather(g, n):
        here = gfin.at[pl.ds(g, n), rows(k * 256, 256)]
        return [send(here, here, {"row": other})]

    z_a = []
    grad_of(2, hid_v, cot)
    core_2 = core_send(2, 1)
    grad_of(0, feat_v, bp)
    core_0 = core_send(0, 1)
    arrived(core_2)
    z_a += z_send(2, 1)
    grad_of(1, fm, bp)
    core_1 = core_send(1, 1)
    arrived(core_0)
    z_a += z_send(0, 1)
    arrived(core_1)
    z_a += z_send(1, 1)
    send_fresh([("row", n) for n in range(ROWS_EARLY, len(ROW_OFFS))])

    arrived(hist_copies)
    aggregate(tab2, sm)
    arrived(z_a)
    xy_a = xy_send(0, 3)
    grad_of(3, sm, cot)
    core_b = core_send(3, 1)
    send_fresh_cols(1)

    for one in hist_copies:
        one.wait_send()
    snd_b[pl.ds(0, BLK), :] = zero_block
    own_slots = [
        pltpu.make_async_copy(snd_b.at[pl.ds(0, BLK)], fresh_h.at[blk(c)], out_sem.at[0]),
        pltpu.make_async_copy(snd_b.at[pl.ds(0, BLK)], fresh_h.at[blk(16 + r)], out_sem.at[1]),
    ]
    for one in own_slots:
        one.start()

    arrived(core_b)
    z_b = z_send(3, 1)
    arrived(xy_a)
    xy_a = xy_gather(0, 3)
    send_fresh_cols(2)

    @pl.loop(0, 4)
    def _(m):
        at = rows(m * 512, 512)
        bm[at, :] = (dot(hid_v[at, :], wts[2]) + dot(sm[at, :], wts[3])).astype(BF)

    emb_copy = pltpu.make_async_copy(bm, emb_h, out_sem.at[2])
    emb_copy.start()

    arrived(z_b)
    xy_b = xy_send(3, 1)
    send_fresh_cols(3)
    arrived(xy_a)
    z_a = z_gather(0, 3)
    arrived(xy_b)
    xy_b = xy_gather(3, 1)
    send_fresh_cols(4)
    arrived(xy_b)
    z_b = z_gather(3, 1)
    arrived(z_a)
    core_a = core_gather(0, 3)
    arrived(z_b)
    core_b = core_gather(3, 1)
    arrived(core_a + core_b)
    grad_copy = pltpu.make_async_copy(gfin, grad_h, out_sem.at[3])
    grad_copy.start()

    for one in fresh_copies:
        one.wait_recv()
    for one in fresh_copies + reduce_copies:
        one.wait_send()
    for one in own_slots:
        one.wait()
    emb_copy.wait()
    grad_copy.wait()


def body(
    features, history, cotangent, adjacency, tile_source, col_sends, col_counts, row_sends, row_counts,
    first_self, first_neigh, second_self, second_neigh,
):
    anyspace = pl.BlockSpec(memory_space=pl.ANY)
    smem = pl.BlockSpec(memory_space=pltpu.SMEM)
    vm = pltpu.VMEM
    dma = pltpu.SemaphoreType.DMA
    emb, fresh, grads = pl.pallas_call(
        kernel,
        out_shape=(
            pltpu.VMEM((LOC, W), BF),
            pltpu.VMEM((24 * BLK, W), BF),
            pltpu.VMEM((4, W, W), BF),
        ),
        in_specs=[anyspace] * 4 + [smem] * 5 + [anyspace] * 4,
        out_specs=(pl.BlockSpec(memory_space=pl.ANY),) * 3,
        scratch_shapes=[
            vm((40 * BLK, W), BF),
            vm((40 * BLK, W), BF),
            vm((LOC, W), BF),
            vm((LOC, W), BF),
            vm((LOC, W), BF),
            vm((N_OFF * BLK, W), BF),
            vm((N_OFF * BLK, W), BF),
            vm((LOC, W), BF),
            vm((RING, BLK * TPB, BLK), BF),
            vm((LOC, TPB * BLK), BF),
            vm((BLK * TPB, BLK), F32),
            vm((LOC, BLK), F32),
            vm((4, W, W), BF),
            vm((LOC, W), BF),
            vm((LOC, W), BF),
            vm((4, W, W), F32),
            vm((LOC, 2 * BLK), BF),
            vm((4, 256, W), F32),
            vm((4, 256, W), BF),
            vm((3, 4, 64, W), BF),
            vm((16, 64, BLK), BF),
            vm((16, 64, BLK), F32),
            vm((15, 64, BLK), BF),
            vm((16, 64, BLK), BF),
            vm((4, W, W), BF),
            dma((8,)), dma((RING,)), dma((4,)),
            dma((N_OFF,)), dma((N_OFF,)), dma((N_OFF,)), dma((N_OFF,)), dma((N_OFF,)), dma((N_OFF,)),
            dma((96,)), dma((96,)),
        ],
        compiler_params=pltpu.CompilerParams(
            collective_id=0, has_side_effects=True, vmem_limit_bytes=54 * 2**20
        ),
        cost_estimate=pl.CostEstimate(flops=18 * 10**9, bytes_accessed=24 * 2**20, transcendentals=2**20),
    )(
        features, history, cotangent, adjacency.reshape(LOC * TPB, BLK), tile_source.T,
        col_sends.reshape(1, -1), col_counts, row_sends.reshape(1, -1), row_counts,
        first_self, first_neigh, second_self, second_neigh,
    )
    return emb, fresh, *(grads[n].astype(F32) for n in range(4))


def solution(mesh):
    nodes = P(("row", "col"), None)
    cube = P(("row", "col"), None, None)
    placed = (nodes, nodes, nodes, cube, nodes, cube, nodes, cube, nodes, P(), P(), P(), P())
    return jax.shard_map(
        body, mesh=mesh, in_specs=placed,
        out_specs=(nodes, nodes, P(), P(), P(), P()), check_vma=False,
    )
```

```python
import functools

import jax
import jax.numpy as jnp
from jax import lax
from jax.experimental import pallas as pl
from jax.experimental.pallas import tpu as pltpu
from jax.sharding import PartitionSpec as P

MESH = pl.DeviceIdType.MESH
BF = jnp.bfloat16
F32 = jnp.float32
BLK = 128
TPB = 8
NB = 16
W = 512
LOC = NB * BLK
RING = 4
ROWS_EARLY = 4
GELU_C = 0.7978845608028654
GELU_A = 0.044715

COL_OFFS = [
    (2, 2), (3, 2), (2, 3), (1, 2), (2, 1), (3, 1), (1, 3), (3, 3), (1, 1),
    (0, 2), (2, 0), (0, 3), (3, 0), (0, 1), (1, 0),
]
ROW_OFFS = [(2, 1), (2, 0), (3, 1), (1, 1), (3, 0), (1, 0), (0, 1)]
N_OFF = len(COL_OFFS) + len(ROW_OFFS)
TURNS = []
for _n in range(len(COL_OFFS)):
    TURNS.append(("col", _n))
    if _n % 2 == 0 and _n // 2 < len(ROW_OFFS):
        TURNS.append(("row", _n // 2))
FRESH_CUTS = (0, 5, 6, 6, 7, 15)


def dot(a, b):
    return jnp.dot(a, b, preferred_element_type=F32)


def dot_nt(a, b):
    return lax.dot_general(a, b, (((1,), (1,)), ((), ())), preferred_element_type=F32)


def dot_tn(a, b):
    return lax.dot_general(a, b, (((0,), (0,)), ((), ())), preferred_element_type=F32)


def blk(i):
    return pl.ds(pl.multiple_of(i * BLK, BLK), BLK)


def rows(i, n):
    return pl.ds(pl.multiple_of(i, n), n)


def kernel(
    feat_h, hist_h, cot_h, adj_h, ts, cs, cc, rs, rc, w1s_h, w1n_h, w2s_h, w2n_h,
    emb_h, fresh_h, grad_h,
    tab1, tab2, feat_v, hid_v, hist_v, snd_a, snd_b, cot, adjr, adjd, scr, deg, wts, fm, bm, acc, strip,
    rv1, s2, rv2, s3, h3, rv3, g3, gfin,
    ld_sem, adj_sem, out_sem, a_ss, a_rs, b_ss, b_rs, f_ss, f_rs, r_ss, r_rs,
):
    bp, sm = hist_v, fm
    c = lax.axis_index("col")
    r = lax.axis_index("row")
    x, y, z, k = c // 4, c % 4, r // 2, r % 2

    loads = [
        pltpu.make_async_copy(src, dst, ld_sem.at[n])
        for n, (src, dst) in enumerate(
            [
                (feat_h, feat_v),
                (hist_h, hist_v),
                (cot_h, cot),
                (w2s_h, wts.at[2]),
                (w2n_h, wts.at[3]),
                (w1s_h, wts.at[0]),
                (w1n_h, wts.at[1]),
                (feat_h, tab1.at[pl.ds(0, LOC)]),
            ]
        )
    ]
    for one in loads:
        one.start()

    def col_of(n, sign=1):
        a, b = COL_OFFS[n]
        dx = (1 - k) * a + k * b
        dy = (1 - k) * b + k * a
        return ((x + 4 + sign * dx) % 4) * 4 + (y + 4 + sign * dy) % 4

    def row_of(n, sign=1):
        a, b = ROW_OFFS[n]
        return ((z + 4 + sign * a) % 4) * 2 + (k + b) % 2

    barrier = pltpu.get_barrier_semaphore()
    for n in range(len(COL_OFFS)):
        pl.semaphore_signal(barrier, 1, device_id={"col": col_of(n)}, device_id_type=MESH)
    for n in range(len(ROW_OFFS)):
        pl.semaphore_signal(barrier, 1, device_id={"row": row_of(n)}, device_id_type=MESH)
    pl.semaphore_wait(barrier, N_OFF)

    def exchange(own, snd, dst, base, ssem, rsem, masked, turns):
        copies = []
        for kind, n in turns:
            turn = n if kind == "col" else len(COL_OFFS) + n
            if kind == "col":
                to = col_of(n)
                which, live = cs[0, to], cc[0, to]
                slot, device = base + c, {"col": to}
            else:
                to = row_of(n)
                which, live = rs[0, to], rc[0, to]
                slot, device = base + 16 + r, {"row": to}
            chosen = own[pl.ds(which * BLK, BLK), :]
            if masked:
                chosen = jnp.where(jnp.full(chosen.shape, live, jnp.int32) > 0, chosen.astype(F32), 0.0)
                chosen = chosen.astype(BF)
            snd[pl.ds(turn * BLK, BLK), :] = chosen
            one = pltpu.make_async_remote_copy(
                src_ref=snd.at[pl.ds(turn * BLK, BLK)],
                dst_ref=dst.at[blk(slot)],
                send_sem=ssem.at[turn],
                recv_sem=rsem.at[turn],
                device_id=device,
                device_id_type=MESH,
            )
            one.start()
            copies.append(one)
        return copies

    loads[0].wait()
    feat_copies = exchange(feat_v, snd_a, tab1, NB, a_ss, a_rs, False, TURNS)
    loads[1].wait()
    hist_copies = exchange(hist_v, snd_b, tab2, NB, b_ss, b_rs, False, TURNS)

    zero_block = jnp.zeros((BLK, W), BF)
    for table in (tab1, tab2):
        table[blk(NB + c), :] = zero_block
        table[blk(NB + 16 + r), :] = zero_block


    def adj_load(i):
        return pltpu.make_async_copy(
            adj_h.at[rows(i * BLK * TPB, BLK * TPB)], adjr.at[i % RING], adj_sem.at[i % RING]
        )

    for i in range(RING):
        adj_load(i).start()

    @pl.loop(0, NB)
    def _(i):
        adj_load(i).wait()
        scr[...] = adjr[i % RING].astype(F32)

        @pl.when(i + RING < NB)
        def _():
            adj_load(i + RING).start()

        total = jnp.zeros((BLK, BLK), F32)
        for t in range(TPB):
            tile = scr[pl.ds(t, BLK, stride=TPB), :]
            adjd[blk(i), pl.ds(t * BLK, BLK)] = tile.astype(BF)
            total += tile
        deg[blk(i), :] = jnp.broadcast_to(jnp.sum(total, axis=1, keepdims=True), (BLK, BLK))

    def divide(v, at):
        d = deg[at, :]
        return v / jnp.concatenate([d] * (W // BLK), axis=1)

    for n in range(2, 8):
        loads[n].wait()

    @pl.loop(0, 8)
    def _(m):
        at = rows(m * 256, 256)
        up = cot[at, :]
        acc[m // 2, rows((m % 2) * 256, 256), :] = dot_nt(up, wts[2])
        bm[at, :] = divide(dot_nt(up, wts[3]), at).astype(BF)

    @pl.loop(0, 8)
    def _(jp):
        @pl.loop(0, NB)
        def _(i):
            for jj in range(2):
                strip_part = jnp.zeros((BLK, BLK), BF)
                for t in range(TPB):
                    source = jnp.full((BLK, BLK), ts[t, i], jnp.int32)
                    hit = jnp.where(source == jp * 2 + jj, 1.0, 0.0).astype(BF)
                    strip_part += hit * adjd[blk(i), pl.ds(t * BLK, BLK)]
                strip[blk(i), pl.ds(jj * BLK, BLK)] = strip_part

        at = rows((jp % 2) * 256, 256)
        acc[jp // 2, at, :] += dot_tn(strip[...], bm[...])

    def aggregate(table, out):
        @pl.loop(0, NB)
        def _(i):
            total = jnp.zeros((BLK, W), F32)
            for t in range(0, TPB, 2):
                pair = jnp.concatenate(
                    [table[pl.ds(ts[t + d, i] * BLK, BLK), :] for d in range(2)], axis=0
                )
                total += dot(adjd[blk(i), pl.ds(t * BLK, 2 * BLK)], pair)
            out[blk(i), :] = divide(total, blk(i)).astype(BF)

    for one in feat_copies:
        one.wait_recv()
    aggregate(tab1, fm)

    @pl.loop(0, 8)
    def _(m):
        at = rows(m * 256, 256)
        v = dot(feat_v[at, :], wts[0]) + dot(fm[at, :], wts[1])
        t = jnp.tanh(GELU_C * (v + GELU_A * (v * v * v)))
        half = 0.5 * (1.0 + t)
        hidden = (v * half).astype(BF)
        hid_v[at, :] = hidden
        tab2[at, :] = hidden
        slope = half + 0.5 * v * (1.0 - t * t) * (GELU_C * (1.0 + 3.0 * GELU_A * (v * v)))
        bp[at, :] = (acc[m // 2, rows((m % 2) * 256, 256), :] * slope).astype(BF)

    for one in feat_copies:
        one.wait_send()
    fresh_copies = []

    def send_fresh(turns):
        fresh_copies.extend(exchange(hid_v, snd_a, fresh_h, 0, f_ss, f_rs, True, turns))

    def send_fresh_cols(part):
        send_fresh([("col", n) for n in range(FRESH_CUTS[part], FRESH_CUTS[part + 1])])

    send_fresh([("row", n) for n in range(ROWS_EARLY)])
    send_fresh_cols(0)

    def grad_of(g, left, right):
        @pl.loop(0, 4)
        def _(q):
            at = rows(q * BLK, BLK)
            acc[g, at, :] = dot_tn(left[:, at], right[...])

    sems = iter(range(96))
    other = z * 2 + 1 - k
    row_base = k * 256 + z * 64
    reduce_copies = []

    def send(src, dst, device):
        n = next(sems)
        one = pltpu.make_async_remote_copy(
            src_ref=src, dst_ref=dst, send_sem=r_ss.at[n], recv_sem=r_rs.at[n],
            device_id=device, device_id_type=MESH,
        )
        one.start()
        reduce_copies.append(one)
        return one

    def arrived(copies):
        for one in copies:
            one.wait_recv()

    def core_send(g, n):
        part = pl.ds(g, n)
        return [send(acc.at[part, rows((1 - k) * 256, 256)], rv1.at[part], {"row": other})]

    def z_send(g, n):
        for p in range(g, g + n):
            at = rows(k * 256, 256)
            both = acc[p, at, :] + rv1[p]
            acc[p, at, :] = both
            s2[p] = both.astype(BF)
        part = pl.ds(g, n)
        copies = []
        for d in range(3):
            zt = (z + d + 1) % 4
            copies.append(send(s2.at[part, rows(zt * 64, 64)], rv2.at[d, part], {"row": zt * 2 + k}))
        return copies

    def xy_send(g, n):
        for p in range(g, g + n):
            total = acc[p, rows(row_base, 64), :]
            for d in range(3):
                total = total + rv2[d, p].astype(F32)
            for d in range(16):
                cut = total[(d // 4) * 16 : (d // 4) * 16 + 16, (d % 4) * BLK : (d % 4) * BLK + BLK]
                h3[d, pl.ds(p * 16, 16), :] = cut
                s3[d, pl.ds(p * 16, 16), :] = cut.astype(BF)
        part = pl.ds(g * 16, n * 16)
        copies = []
        for m in range(len(COL_OFFS)):
            to = col_of(m)
            copies.append(send(s3.at[to, part], rv3.at[m, part], {"col": to}))
        return copies

    def xy_gather(g, n):
        part = pl.ds(g * 16, n * 16)
        total = h3[c, part, :]
        for m in range(len(COL_OFFS)):
            total = total + rv3[m, part, :].astype(F32)
        g3[c, part, :] = total.astype(BF)
        here = g3.at[c, part]
        return [send(here, here, {"col": col_of(m)}) for m in range(len(COL_OFFS))]

    def z_gather(g, n):
        for p in range(g, g + n):
            for d in range(16):
                at = rows(row_base + (d // 4) * 16, 16)
                gfin[p, at, pl.ds((d % 4) * BLK, BLK)] = g3[d, pl.ds(p * 16, 16), :]
        here = gfin.at[pl.ds(g, n), rows(row_base, 64)]
        return [send(here, here, {"row": ((z + d + 1) % 4) * 2 + k}) for d in range(3)]

    def core_gather(g, n):
        here = gfin.at[pl.ds(g, n), rows(k * 256, 256)]
        return [send(here, here, {"row": other})]

    z_a = []
    grad_of(2, hid_v, cot)
    core_2 = core_send(2, 1)
    grad_of(0, feat_v, bp)
    core_0 = core_send(0, 1)
    arrived(core_2)
    z_a += z_send(2, 1)
    grad_of(1, fm, bp)
    core_1 = core_send(1, 1)
    arrived(core_0)
    z_a += z_send(0, 1)
    arrived(core_1)
    z_a += z_send(1, 1)
    send_fresh([("row", n) for n in range(ROWS_EARLY, len(ROW_OFFS))])

    arrived(hist_copies)
    aggregate(tab2, sm)
    arrived(z_a)
    xy_a = xy_send(0, 3)
    grad_of(3, sm, cot)
    core_b = core_send(3, 1)
    send_fresh_cols(1)

    for one in hist_copies:
        one.wait_send()
    snd_b[pl.ds(0, BLK), :] = zero_block
    own_slots = [
        pltpu.make_async_copy(snd_b.at[pl.ds(0, BLK)], fresh_h.at[blk(c)], out_sem.at[0]),
        pltpu.make_async_copy(snd_b.at[pl.ds(0, BLK)], fresh_h.at[blk(16 + r)], out_sem.at[1]),
    ]
    for one in own_slots:
        one.start()

    arrived(core_b)
    z_b = z_send(3, 1)
    arrived(xy_a)
    xy_a = xy_gather(0, 3)
    send_fresh_cols(2)

    @pl.loop(0, 4)
    def _(m):
        at = rows(m * 512, 512)
        bm[at, :] = (dot(hid_v[at, :], wts[2]) + dot(sm[at, :], wts[3])).astype(BF)

    emb_copy = pltpu.make_async_copy(bm, emb_h, out_sem.at[2])
    emb_copy.start()

    arrived(z_b)
    xy_b = xy_send(3, 1)
    send_fresh_cols(3)
    arrived(xy_a)
    z_a = z_gather(0, 3)
    arrived(xy_b)
    xy_b = xy_gather(3, 1)
    send_fresh_cols(4)
    arrived(xy_b)
    z_b = z_gather(3, 1)
    arrived(z_a)
    core_a = core_gather(0, 3)
    arrived(z_b)
    core_b = core_gather(3, 1)
    grad_copies = []
    for g, n, last in ((0, 3, core_a), (3, 1, core_b)):
        arrived(last)
        part = pl.ds(g, n)
        grad_copies.append(pltpu.make_async_copy(gfin.at[part], grad_h.at[part], out_sem.at[3 + g // 3]))
        grad_copies[-1].start()

    for one in fresh_copies:
        one.wait_recv()
    for one in fresh_copies + reduce_copies:
        one.wait_send()
    for one in own_slots:
        one.wait()
    emb_copy.wait()
    for one in grad_copies:
        one.wait()


def body(
    features, history, cotangent, adjacency, tile_source, col_sends, col_counts, row_sends, row_counts,
    first_self, first_neigh, second_self, second_neigh,
):
    anyspace = pl.BlockSpec(memory_space=pl.ANY)
    smem = pl.BlockSpec(memory_space=pltpu.SMEM)
    vm = pltpu.VMEM
    dma = pltpu.SemaphoreType.DMA
    emb, fresh, grads = pl.pallas_call(
        kernel,
        out_shape=(
            pltpu.VMEM((LOC, W), BF),
            pltpu.VMEM((24 * BLK, W), BF),
            pltpu.VMEM((4, W, W), BF),
        ),
        in_specs=[anyspace] * 4 + [smem] * 5 + [anyspace] * 4,
        out_specs=(pl.BlockSpec(memory_space=pl.ANY),) * 3,
        scratch_shapes=[
            vm((40 * BLK, W), BF),
            vm((40 * BLK, W), BF),
            vm((LOC, W), BF),
            vm((LOC, W), BF),
            vm((LOC, W), BF),
            vm((N_OFF * BLK, W), BF),
            vm((N_OFF * BLK, W), BF),
            vm((LOC, W), BF),
            vm((RING, BLK * TPB, BLK), BF),
            vm((LOC, TPB * BLK), BF),
            vm((BLK * TPB, BLK), F32),
            vm((LOC, BLK), F32),
            vm((4, W, W), BF),
            vm((LOC, W), BF),
            vm((LOC, W), BF),
            vm((4, W, W), F32),
            vm((LOC, 2 * BLK), BF),
            vm((4, 256, W), F32),
            vm((4, 256, W), BF),
            vm((3, 4, 64, W), BF),
            vm((16, 64, BLK), BF),
            vm((16, 64, BLK), F32),
            vm((15, 64, BLK), BF),
            vm((16, 64, BLK), BF),
            vm((4, W, W), BF),
            dma((8,)), dma((RING,)), dma((5,)),
            dma((N_OFF,)), dma((N_OFF,)), dma((N_OFF,)), dma((N_OFF,)), dma((N_OFF,)), dma((N_OFF,)),
            dma((96,)), dma((96,)),
        ],
        compiler_params=pltpu.CompilerParams(
            collective_id=0, has_side_effects=True, vmem_limit_bytes=54 * 2**20
        ),
        cost_estimate=pl.CostEstimate(flops=18 * 10**9, bytes_accessed=24 * 2**20, transcendentals=2**20),
    )(
        features, history, cotangent, adjacency.reshape(LOC * TPB, BLK), tile_source.T,
        col_sends.reshape(1, -1), col_counts, row_sends.reshape(1, -1), row_counts,
        first_self, first_neigh, second_self, second_neigh,
    )
    return emb, fresh, *(grads[n].astype(F32) for n in range(4))


def solution(mesh):
    nodes = P(("row", "col"), None)
    cube = P(("row", "col"), None, None)
    placed = (nodes, nodes, nodes, cube, nodes, cube, nodes, cube, nodes, P(), P(), P(), P())
    return jax.shard_map(
        body, mesh=mesh, in_specs=placed,
        out_specs=(nodes, nodes, P(), P(), P(), P()), check_vma=False,
    )
```
